256 devices in a mesh: frame: 32 (over y_hi, z, core), fsdp: 8 (over y_lo, x).
Axes of the slice: x: 4, y: 4 (y_hi: 2, y_lo: 2; y = y_hi * 2 + y_lo), z: 8, core: 2. Of those that a mesh axis runs over, the one named last changes fastest.
Arguments:
- latent_tokens: bfloat16 [12288, 1536], P(('frame', 'fsdp')), may hold values from -6 to 6
- level_index: int32 [32], P('frame'), may hold values from 0 to 999
- timestep_table: int32 [1000], replicated, may hold values from 0 to 999
- time_weight: float32 [256, 9216], P(None, 'fsdp'), may hold values from -0.375 to 0.375
- block_mod: float32 [6, 1536], replicated, may hold values from -2 to 2
- w_query: bfloat16 [1536, 1024], P(None, 'fsdp'), may hold values from -1.5309311 to 1.5309311
- w_key: bfloat16 [1536, 1024], P(None, 'fsdp'), may hold values from -1.5309311 to 1.5309311
- w_value: bfloat16 [1536, 1024], P(None, 'fsdp'), may hold values from -0.15625 to 0.15625
- q_gain: float32 [1024], P('fsdp'), may hold values from 0.5 to 6
- k_gain: float32 [1024], P('fsdp'), may hold values from 0.5 to 6
- w_out: bfloat16 [1024, 1536], P('fsdp'), may hold values from -0.1875 to 0.1875
- w_up: bfloat16 [1536, 8960], P(None, 'fsdp'), may hold values from -0.15625 to 0.15625
- w_down: bfloat16 [8960, 1536], P('fsdp'), may hold values from -0.0625 to 0.0625
Outputs:
- rolled: bfloat16 [12288, 1536], P(('frame', 'fsdp'))
The draws below stay inside these ranges and needn't reach their ends.
All inputs are finite; a program needn't handle non-finite values.
Results may differ from the reference program's by a relative error of at most 0.014.
Values may be sent and summed in bfloat16 or wider, within the bound.
No kernel may reach another device: no remote copies, remote signals or barrier semaphores. Data moves between devices by JAX's collectives and lax.ppermute only.
A program may use at most 64 MiB of HBM per device.

```python
import math
import jax
import jax.numpy as jnp
from jax import lax

D = 1536
FF = 8960
HEAD_DIM = 128
FREQ = 256
HEADS = 8
LEVELS = 1000
GRID_W = 24
TPF = 384
FRAMES = 32
N_FRAME = 32
N_FSDP = 8


def query_base(key):
    return jax.random.truncated_normal(key, -6.0, 6.0, (D, HEADS * HEAD_DIM), jnp.float32)


def head_ramp(highest):
    head_of = jnp.arange(HEADS * HEAD_DIM) // HEAD_DIM
    return highest ** (head_of.astype(jnp.float32) / max(HEADS - 1, 1))


def draw_w_query(key, part):
    base = query_base(key)
    ramp = head_ramp(3.0)
    return (base * ramp[None, :] * D ** (-0.5)).astype(jnp.bfloat16)


def draw_w_key(key, part):
    key = jax.random.fold_in(key, 12)
    fresh = jax.random.truncated_normal(key, -6.0, 6.0, (D, HEADS * HEAD_DIM), jnp.float32)
    mixed = fresh
    ramp = head_ramp(3.0)
    return (mixed * ramp[None, :] * D ** (-0.5)).astype(jnp.bfloat16)


def gain_values(key):
    return jax.random.uniform(key, (HEADS * HEAD_DIM,), jnp.float32, 0.5, 1.5)


def draw_q_gain(key, part):
    key = jax.random.fold_in(key, 13)
    return gain_values(key)


def draw_k_gain(key, part):
    key = jax.random.fold_in(key, 14)
    return gain_values(key)


def set_ends(drawn, stream_key, low, high):
    extent = drawn.shape
    place = [jax.random.randint(jax.random.fold_in(stream_key, axis), (), 0, extent[axis]) for axis in range(len(extent))]
    drawn = drawn.at[tuple(place)].set(low)
    longest = extent.index(max(extent))
    place[longest] = (place[longest] + 1) % extent[longest]
    return drawn.at[tuple(place)].set(high)


def shard_levels(stream_key, shape, split, smallest, top_value):
    gain = 1.0
    for dim, blocks in split:
        draws = jax.random.uniform(jax.random.fold_in(jax.random.fold_in(stream_key, 6), dim), (blocks,), jnp.float32, smallest / len(split), top_value / len(split))
        gain = gain * jnp.repeat(jnp.exp(draws), shape[dim] // blocks).reshape((-1,) + (1,) * (len(shape) - 1 - dim))
    return gain


def normal_values(rng, dims, scale, limit, pieces=(), kind=jnp.bfloat16):
    gain = shard_levels(rng, dims, pieces, -0.22, 0.18) if pieces else 1.0
    drawn = jax.random.normal(rng, dims, jnp.float32) * scale * gain
    return jnp.minimum(jnp.maximum(drawn, -limit), limit).astype(kind)


def setup_inputs(seed: int = 0) -> dict:
    keys = jax.random.split(jax.random.key(seed), 14)
    return {
        "latent_tokens": normal_values(keys[0], (FRAMES * TPF, D), 1.0, 6.0, ((0, 256),)),
        "level_index": set_ends(jax.random.randint(keys[1], (FRAMES,), 0, LEVELS), jax.random.fold_in(keys[1], 1), 0, LEVELS - 1).astype(jnp.int32),
        "timestep_table": set_ends(jax.random.randint(keys[2], (LEVELS,), 0, 1000), jax.random.fold_in(keys[2], 1), 0, 999).astype(jnp.int32),
        "time_weight": normal_values(keys[3], (FREQ, 6 * D), FREQ ** -0.5, 0.375, ((1, 8),), jnp.float32),
        "block_mod": normal_values(keys[4], (6, D), 0.3, 2.0, (), jnp.float32),
        "w_query": draw_w_query(jax.random.fold_in(keys[13], 71), 0),
        "w_key": draw_w_key(jax.random.fold_in(keys[13], 71), 0),
        "w_value": normal_values(keys[7], (D, HEADS * HEAD_DIM), D ** -0.5, 0.15625, ((1, 8),)),
        "q_gain": draw_q_gain(jax.random.fold_in(keys[13], 71), 0),
        "k_gain": draw_k_gain(jax.random.fold_in(keys[13], 71), 0),
        "w_out": normal_values(keys[10], (HEADS * HEAD_DIM, D), (HEADS * HEAD_DIM) ** -0.5, 0.1875, ((0, 8),)),
        "w_up": normal_values(keys[11], (D, FF), D ** -0.5, 0.15625, ((1, 8),)),
        "w_down": normal_values(keys[12], (FF, D), FF ** -0.5, 0.0625, ((0, 8),)),
    }


EPS_NORM = 1e-06

def sinusoid(times):
    halfway = FREQ // 2
    frequency = jnp.exp(-math.log(10000.0) * jnp.arange(halfway, dtype=jnp.float32) / halfway)
    product = times[:, None] * frequency[None, :]
    return jnp.concatenate([jnp.cos(product), jnp.sin(product)], axis=1)

def rope_angles(frame_pos, token_pos):
    halfway = HEAD_DIM // 2
    spatial = HEAD_DIM // 6
    temporal = halfway - 2 * spatial
    pair_index = jnp.arange(halfway, dtype=jnp.int32)
    local_index = jnp.where(pair_index < temporal, pair_index, jnp.where(pair_index < temporal + spatial, pair_index - temporal, pair_index - temporal - spatial))
    span = jnp.where(pair_index < temporal, 2 * temporal, 2 * spatial)
    frequency = jnp.exp(-math.log(10000.0) * 2.0 * local_index.astype(jnp.float32) / span.astype(jnp.float32))
    height = (token_pos // GRID_W).astype(jnp.float32)
    across = (token_pos % GRID_W).astype(jnp.float32)
    timing = frame_pos.astype(jnp.float32)
    position = jnp.where(pair_index[None, :] < temporal, timing[:, None], jnp.where(pair_index[None, :] < temporal + spatial, height[:, None], across[:, None]))
    return position * frequency[None, :]

def apply_rope(features, angles):
    row_count, columns = features.shape
    halfway = HEAD_DIM // 2
    shaped = features.reshape(row_count, columns // HEAD_DIM, HEAD_DIM)
    first_half = shaped[..., :halfway]
    second_half = shaped[..., halfway:]
    cosine = jnp.cos(angles)[:, None, :]
    sine = jnp.sin(angles)[:, None, :]
    turned = jnp.concatenate([first_half * cosine - second_half * sine, first_half * sine + second_half * cosine], axis=-1)
    return turned.reshape(row_count, columns)

def layer_norm(values):
    center = lax.optimization_barrier(jnp.mean(values, axis=-1, keepdims=True))
    shifted = values - center
    spread = lax.optimization_barrier(jnp.mean(shifted * shifted, axis=-1, keepdims=True))
    return shifted * lax.rsqrt(spread + EPS_NORM)

def modulate(values, shift_row, scale_row):
    return layer_norm(values) * (1.0 + scale_row) + shift_row

def split_sum(left_side, right_side, piece_count):
    piece_width = left_side.shape[1] // piece_count
    running = jnp.zeros((left_side.shape[0], right_side.shape[1]), jnp.float32)
    for group_index in range(piece_count):
        lower = group_index * piece_width
        product = jnp.dot(left_side[:, lower:lower + piece_width], right_side[lower:lower + piece_width], preferred_element_type=jnp.float32)
        running = running + lax.optimization_barrier(product.astype(jnp.bfloat16)).astype(jnp.float32)
    return running

def reference(latent_tokens, level_index, timestep_table, time_weight, block_mod, w_query, w_key, w_value, q_gain, k_gain, w_out, w_up, w_down):
    frames = N_FRAME
    full_width = HEADS * HEAD_DIM
    step_time = timestep_table[level_index].astype(jnp.float32)
    embedded = sinusoid(step_time)
    modulation = jnp.dot(jax.nn.silu(embedded), time_weight, precision=lax.Precision.HIGHEST).reshape(frames, 6, D) + block_mod[None]
    hidden_in = latent_tokens.astype(jnp.float32).reshape(frames, TPF, D)
    first_in = modulate(hidden_in, modulation[:, 0:1], modulation[:, 1:2]).astype(jnp.bfloat16).reshape(frames * TPF, D)
    query_raw = jnp.dot(first_in, w_query, preferred_element_type=jnp.float32)
    key_raw = jnp.dot(first_in, w_key, preferred_element_type=jnp.float32)
    value_raw = jnp.dot(first_in, w_value, preferred_element_type=jnp.float32)
    frame_pos = jnp.repeat(jnp.arange(frames, dtype=jnp.int32), TPF)
    token_pos = jnp.tile(jnp.arange(TPF, dtype=jnp.int32), frames)
    angles = rope_angles(frame_pos, token_pos)
    query_scale = lax.rsqrt(lax.optimization_barrier(jnp.mean(query_raw * query_raw, axis=1, keepdims=True)) + EPS_NORM)
    key_scale = lax.rsqrt(lax.optimization_barrier(jnp.mean(key_raw * key_raw, axis=1, keepdims=True)) + EPS_NORM)
    queries = apply_rope(query_raw * query_scale * q_gain[None, :], angles).astype(jnp.bfloat16)
    key_rows = apply_rope(key_raw * key_scale * k_gain[None, :], angles).astype(jnp.bfloat16)
    values = value_raw.astype(jnp.bfloat16)
    key_heads = key_rows.reshape(frames * TPF, HEADS, HEAD_DIM).astype(jnp.float32)
    value_heads = values.reshape(frames * TPF, HEADS, HEAD_DIM).astype(jnp.float32)

    def one_frame(frame_index):
        query_block = lax.dynamic_slice_in_dim(queries, (frame_index * TPF).astype(jnp.int32), TPF, 0)
        query_block = query_block.reshape(TPF, HEADS, HEAD_DIM).astype(jnp.float32)
        scores = jnp.einsum('qhd,khd->hqk', query_block, key_heads) * HEAD_DIM ** (-0.5)
        scores = jnp.where(frame_pos[None, None, :] <= frame_index, scores, -jnp.inf)
        row_max = lax.optimization_barrier(jnp.max(scores, axis=-1, keepdims=True))
        probs = jnp.exp(scores - row_max)
        row_total = lax.optimization_barrier(jnp.sum(probs, axis=-1, keepdims=True))
        weights = lax.optimization_barrier(probs.astype(jnp.bfloat16)).astype(jnp.float32)
        summed = jnp.einsum('hqk,khd->hqd', weights, value_heads) / row_total
        return jnp.transpose(summed, (1, 0, 2)).reshape(TPF, full_width).astype(jnp.bfloat16)
    attended = lax.map(one_frame, jnp.arange(frames, dtype=jnp.int32)).reshape(frames * TPF, full_width)
    attn_sum = split_sum(attended, w_out, N_FSDP).reshape(frames, TPF, D)
    after_attn = hidden_in + modulation[:, 2:3] * attn_sum
    second_in = modulate(after_attn, modulation[:, 3:4], modulation[:, 4:5]).astype(jnp.bfloat16).reshape(frames * TPF, D)
    expanded = jax.nn.gelu(jnp.dot(second_in, w_up, preferred_element_type=jnp.float32), approximate=True).astype(jnp.bfloat16)
    mlp_sum = split_sum(expanded, w_down, N_FSDP).reshape(frames, TPF, D)
    block_out = (after_attn + modulation[:, 5:6] * mlp_sum).astype(jnp.bfloat16)
    return jnp.roll(block_out, 1, axis=0).reshape(frames * TPF, D)
```

```python
import functools
import math

import jax
import jax.numpy as jnp
from jax import lax
from jax.experimental import pallas as pl
from jax.experimental.pallas import tpu as pltpu
from jax.sharding import PartitionSpec as P

HEAD_DIM = 128
HALF = HEAD_DIM // 2
FREQ = 256
GRID_W = 24
EPS_NORM = 1e-06

Y_HI, Z, CORE = 2, 8, 2
Y_LO, X = 2, 4
FRAMES = Y_HI * Z * CORE
GROUPS = Y_LO * X
SHIFTS = tuple((a, b) for a in range(Y_LO) for b in range(X))
MATES = ((0, 0), (0, 1), (1, 0), (1, 1))
LOG2E = math.log2(math.e)
NEVER = -1e30
STAT_ROWS = 16
VMEM_LIMIT = 50 * 1024 * 1024

BF16 = jnp.bfloat16
F32 = jnp.float32


def params():
    return pltpu.CompilerParams(vmem_limit_bytes=VMEM_LIMIT)


def vmem(count):
    return [pl.BlockSpec(memory_space=pltpu.VMEM)] * count


def smem():
    return pl.BlockSpec(memory_space=pltpu.SMEM)


def move(array, target):
    pairs = []
    for frame in range(FRAMES):
        for part in range(GROUPS):
            to_frame, to_part = target(frame, part)
            pairs.append((frame * GROUPS + part, to_frame * GROUPS + to_part))
    return lax.ppermute(array, ("frame", "fsdp"), pairs)


def group_shift(part, a, b):
    y, x = divmod(part, X)
    return (y ^ a) * X + (x + b) % X


def frame_shift(frame, dy, dz, dc):
    core = frame % CORE
    z = (frame // CORE) % Z
    y = frame // (CORE * Z)
    return ((y ^ dy) * Z + (z + dz) % Z) * CORE + (core ^ dc)


def from_group(array, a, b):
    return move(array, lambda f, s: (f, group_shift(s, a, -b)))


def from_frame(array, dy, dz, dc):
    return move(array, lambda f, s: (frame_shift(f, dy, -dz, dc), s))


def to_next_frame(array, a, b):
    return move(array, lambda f, s: ((f + 1) % FRAMES, group_shift(s, a, b)))


def sinusoid(times):
    halfway = FREQ // 2
    frequency = jnp.exp(-math.log(10000.0) * jnp.arange(halfway, dtype=F32) / halfway)
    product = times[:, None] * frequency[None, :]
    return jnp.concatenate([jnp.cos(product), jnp.sin(product)], axis=1)


def rope_angles(frame_pos, token_pos):
    spatial = HEAD_DIM // 6
    temporal = HALF - 2 * spatial
    pair_index = jnp.arange(HALF, dtype=jnp.int32)
    local_index = jnp.where(
        pair_index < temporal,
        pair_index,
        jnp.where(
            pair_index < temporal + spatial, pair_index - temporal, pair_index - temporal - spatial
        ),
    )
    span = jnp.where(pair_index < temporal, 2 * temporal, 2 * spatial)
    frequency = jnp.exp(-math.log(10000.0) * 2.0 * local_index.astype(F32) / span.astype(F32))
    height = (token_pos // GRID_W).astype(F32)
    across = (token_pos % GRID_W).astype(F32)
    timing = frame_pos.astype(F32)
    index = pair_index[:, None]
    position = jnp.where(
        index < temporal,
        timing[None, :],
        jnp.where(index < temporal + spatial, height[None, :], across[None, :]),
    )
    return position * frequency[:, None]


def normalized(values):
    center = jnp.mean(values, axis=-1, keepdims=True)
    shifted = values - center
    spread = jnp.mean(shifted * shifted, axis=-1, keepdims=True)
    return shifted * lax.rsqrt(spread + EPS_NORM)


def project_kernel(place, *refs):
    pieces = refs[:GROUPS]
    mod, w_query, w_key, w_value, tables = refs[GROUPS : GROUPS + 5]
    query_out, key_out, value_out, squares_out, rows = refs[GROUPS + 5 :]
    tok = pieces[0].shape[0]
    shift_row = mod[0:1, :]
    scale_row = 1.0 + mod[1:2, :]
    for slot in range(GROUPS):
        values = pieces[slot][...].astype(F32)
        start = pl.multiple_of(place[slot] * tok, tok)
        rows[pl.ds(start, tok), :] = (normalized(values) * scale_row + shift_row).astype(BF16)
    block = rows[...]
    value_raw = jnp.dot(block, w_value[...], preferred_element_type=F32)
    value_out[...] = value_raw.T.astype(BF16)
    found = []
    for kind, (weight, out) in enumerate(((w_query, query_out), (w_key, key_out))):
        raw = jnp.dot(block, weight[...], preferred_element_type=F32).T
        found.append(jnp.sum(raw * raw, axis=0, keepdims=True))
        first, second = raw[:HALF], raw[HALF:]
        out[:HALF, :] = first * tables[kind, 0] - second * tables[kind, 1]
        out[HALF:, :] = first * tables[kind, 2] + second * tables[kind, 3]
    per_frame = block.shape[0]
    both = jnp.concatenate(found + [jnp.zeros((6, per_frame), F32)], axis=0)
    for group in range(GROUPS):
        squares_out[group * 8 : group * 8 + 8, :] = both


def scale_kernel(squares, query_raw, key_raw, query_out, key_out):
    total = squares[0:8, :]
    for group in range(1, GROUPS):
        total = total + squares[group * 8 : group * 8 + 8, :]
    scale = lax.rsqrt(total / (GROUPS * HEAD_DIM) + EPS_NORM)
    query_out[...] = (query_raw[...] * (scale[0:1] * (LOG2E * HEAD_DIM ** (-0.5)))).astype(BF16)
    key_out[...] = (key_raw[...] * scale[1:2]).T.astype(BF16)


def attend_kernel(blocks, first, last, frames, *refs):
    query_refs = refs[:4]
    key_refs = refs[4 : 4 + blocks]
    value_refs = refs[4 + blocks : 4 + 2 * blocks]
    rest = refs[4 + 2 * blocks :]
    if not first:
        stat_in, acc_in = rest[:2]
        rest = rest[2:]
    if last:
        packed = rest[:4]
        stat, acc = rest[4:]
    else:
        stat, acc = rest
    if first:
        stat[0:4, :] = jnp.full_like(stat[0:4, :], NEVER)
        stat[4:8, :] = jnp.zeros_like(stat[4:8, :])
        acc[...] = jnp.zeros_like(acc)
    else:
        stat[...] = stat_in[...]
        acc[...] = acc_in[...]
    for slot in range(4):
        for block in range(blocks):

            @pl.when(frames[4 + block] <= frames[slot])
            def _():
                rows = slice(slot * HEAD_DIM, (slot + 1) * HEAD_DIM)
                scores = jnp.dot(
                    key_refs[block][...], query_refs[slot][...], preferred_element_type=F32
                )
                old_max = stat[slot : slot + 1, :]
                new_max = jnp.maximum(old_max, jnp.max(scores, axis=0, keepdims=True))
                decay = jnp.exp2(old_max - new_max)
                probs = jnp.exp2(scores - new_max)
                stat[4 + slot : 5 + slot, :] = stat[4 + slot : 5 + slot, :] * decay + jnp.sum(
                    probs, axis=0, keepdims=True
                )
                stat[slot : slot + 1, :] = new_max
                acc[rows, :] = acc[rows, :] * decay + jnp.dot(
                    value_refs[block][...], probs.astype(BF16), preferred_element_type=F32
                )

    if last:
        for slot in range(4):
            total = stat[4 + slot : 5 + slot, :]
            seen = total > 0.0
            safe = jnp.where(seen, total, 1.0)
            level = jnp.where(seen, stat[slot : slot + 1, :] + jnp.log2(safe), NEVER)
            rows = slice(slot * HEAD_DIM, (slot + 1) * HEAD_DIM)
            packed[slot][0:HEAD_DIM, :] = (acc[rows, :] / safe).astype(BF16)
            high = level.astype(BF16).astype(F32)
            middle = (level - high).astype(BF16).astype(F32)
            low = level - high - middle
            filler = jnp.zeros((STAT_ROWS - 3, level.shape[1]), F32)
            packed[slot][HEAD_DIM:, :] = jnp.concatenate(
                [high, middle, low, filler], axis=0
            ).astype(BF16)


def merge_kernel(*refs):
    packed, out = refs[:4], refs[4]
    levels = []
    for ref in packed:
        parts = ref[HEAD_DIM:, :].astype(F32)
        levels.append(parts[0:1] + parts[1:2] + parts[2:3])
    highest = functools.reduce(jnp.maximum, levels)
    shares = [jnp.exp2(level - highest) for level in levels]
    total = functools.reduce(lambda p, q: p + q, shares)
    mixed = functools.reduce(
        lambda p, q: p + q,
        [ref[:HEAD_DIM, :].astype(F32) * share for ref, share in zip(packed, shares)],
    )
    out[...] = (mixed / total).T.astype(BF16)


HIDDEN_STEP = 384


def mlp_kernel(place, *refs):
    heads = refs[:GROUPS]
    pieces = refs[GROUPS : 2 * GROUPS]
    mod, w_out, w_up, w_down = refs[2 * GROUPS : 2 * GROUPS + 4]
    outs = refs[2 * GROUPS + 4 : 3 * GROUPS + 4]
    attended, after, second, total, out_vm, up_vm, down_vm, sems = refs[3 * GROUPS + 4 :]
    copies = [
        pltpu.make_async_copy(source, target, sems.at[index])
        for index, (source, target) in enumerate(
            ((w_out, out_vm), (w_up, up_vm), (w_down, down_vm))
        )
    ]
    for copy in copies:
        copy.start()
    tok = pieces[0].shape[0]
    for slot in range(GROUPS):
        column = pl.multiple_of(place[slot] * HEAD_DIM, HEAD_DIM)
        attended[:, pl.ds(column, HEAD_DIM)] = heads[slot][...]
    copies[0].wait()
    total[...] = jnp.dot(attended[...], out_vm[...], preferred_element_type=F32)
    gate = mod[2:3, :]
    shift_row = mod[3:4, :]
    scale_row = 1.0 + mod[4:5, :]
    for slot in range(GROUPS):
        rows = pl.ds(pl.multiple_of(place[slot] * tok, tok), tok)
        summed = pieces[slot][...].astype(F32) + gate * total[rows, :]
        if slot == 0:
            after[...] = summed
        second[rows, :] = (normalized(summed) * scale_row + shift_row).astype(BF16)
    copies[1].wait()
    hidden = up_vm.shape[1]
    for index, low in enumerate(range(0, hidden, HIDDEN_STEP)):
        high = min(low + HIDDEN_STEP, hidden)
        inner = jax.nn.gelu(
            jnp.dot(second[...], up_vm[:, low:high], preferred_element_type=F32), approximate=True
        ).astype(BF16)
        if index == 0:
            copies[2].wait()
        product = jnp.dot(inner, down_vm[low:high, :], preferred_element_type=F32)
        if index == 0:
            total[...] = product
        else:
            total[...] += product
    last_gate = mod[5:6, :]
    for slot in range(GROUPS):
        rows = pl.ds(pl.multiple_of(place[slot] * tok, tok), tok)
        share = last_gate * total[rows, :]
        if slot == 0:
            outs[slot][...] = after[...] + share
        else:
            outs[slot][...] = share.astype(BF16)


def local(
    latent_tokens,
    level_index,
    timestep_table,
    time_weight,
    block_mod,
    w_query,
    w_key,
    w_value,
    q_gain,
    k_gain,
    w_out,
    w_up,
    w_down,
):
    frame_id = lax.axis_index("frame")
    part_id = lax.axis_index("fsdp")
    tok, width = latent_tokens.shape
    per_frame = tok * GROUPS
    hidden = w_up.shape[1]
    my_y, my_x = part_id // X, part_id % X
    place = jnp.stack([(my_y ^ a) * X + (my_x + b) % X for a, b in SHIFTS]).astype(jnp.int32)

    pieces = [latent_tokens] + [from_group(latent_tokens, a, b) for a, b in SHIFTS[1:]]

    picked = jnp.arange(timestep_table.shape[0], dtype=jnp.int32) == level_index[0]
    step_time = jnp.sum(jnp.where(picked, timestep_table, 0)).astype(F32)
    embedded = sinusoid(step_time[None])
    mod_part = jnp.dot(jax.nn.silu(embedded), time_weight, precision=lax.Precision.HIGHEST)
    mod_all = lax.all_to_all(
        jnp.broadcast_to(mod_part, (GROUPS, mod_part.shape[1])), "fsdp", 0, 0, tiled=True
    )
    modulation = mod_all.reshape(6, width) + block_mod

    token_pos = jnp.arange(per_frame, dtype=jnp.int32)
    angles = rope_angles(jnp.full((per_frame,), frame_id, jnp.int32), token_pos)
    cosine, sine = jnp.cos(angles), jnp.sin(angles)
    tables = jnp.stack(
        [
            jnp.stack(
                [
                    gain[:HALF, None] * cosine,
                    gain[HALF:, None] * sine,
                    gain[:HALF, None] * sine,
                    gain[HALF:, None] * cosine,
                ]
            )
            for gain in (q_gain, k_gain)
        ]
    )

    query_raw, key_raw, value_t, squares = pl.pallas_call(
        project_kernel,
        out_shape=(
            jax.ShapeDtypeStruct((HEAD_DIM, per_frame), F32),
            jax.ShapeDtypeStruct((HEAD_DIM, per_frame), F32),
            jax.ShapeDtypeStruct((HEAD_DIM, per_frame), BF16),
            jax.ShapeDtypeStruct((GROUPS * 8, per_frame), F32),
        ),
        in_specs=[smem()] + vmem(GROUPS + 5),
        out_specs=tuple(vmem(4)),
        scratch_shapes=[pltpu.VMEM((per_frame, width), BF16)],
        compiler_params=params(),
        name="project",
    )(place, *pieces, modulation, w_query, w_key, w_value, tables)

    w_out_after, squares = lax.optimization_barrier((w_out, squares))
    w_out_full = lax.all_gather(w_out_after, "fsdp", axis=0, tiled=True)

    squares = lax.all_to_all(squares, "fsdp", 0, 0, tiled=True)
    query_t, key_rows = pl.pallas_call(
        scale_kernel,
        out_shape=(
            jax.ShapeDtypeStruct((HEAD_DIM, per_frame), BF16),
            jax.ShapeDtypeStruct((per_frame, HEAD_DIM), BF16),
        ),
        in_specs=vmem(3),
        out_specs=tuple(vmem(2)),
        compiler_params=params(),
        name="scale",
    )(squares, query_raw, key_raw)

    queries = [query_t] + [from_frame(query_t, dy, 0, dc) for dy, dc in MATES[1:]]
    keys = {0: key_rows}
    values = {0: value_t}
    for step in range(1, Z // 2):
        for sign in (1, -1):
            keys[sign * step] = from_frame(keys[sign * (step - 1)], 0, sign, 0)
            values[sign * step] = from_frame(values[sign * (step - 1)], 0, sign, 0)
    far = Z // 2
    keys[far] = from_frame(keys[far - 1], 0, 1, 0)
    values[far] = from_frame(values[1 - far], 0, -1, 0)

    core = frame_id % CORE
    my_z = (frame_id // CORE) % Z
    my_yhi = frame_id // (CORE * Z)
    query_frames = [((my_yhi ^ dy) * Z + my_z) * CORE + (core ^ dc) for dy, dc in MATES]

    def key_frame(offset):
        return (my_yhi * Z + (my_z + offset) % Z) * CORE + core

    stat_shape = jax.ShapeDtypeStruct((8, per_frame), F32)
    acc_shape = jax.ShapeDtypeStruct((4 * HEAD_DIM, per_frame), F32)
    packed_shape = jax.ShapeDtypeStruct((HEAD_DIM + STAT_ROWS, per_frame), BF16)
    state = ()
    plan = [(0, 1, -1), (2, -2), (3, -3), (far,)]
    for index, offsets in enumerate(plan):
        first, last = index == 0, index == len(plan) - 1
        count = len(offsets)
        frames = jnp.stack(query_frames + [key_frame(o) for o in offsets]).astype(jnp.int32)
        operands = (
            [frames]
            + queries
            + [keys[o] for o in offsets]
            + [values[o] for o in offsets]
            + list(state)
        )
        work = 4 * count * per_frame * per_frame
        state = pl.pallas_call(
            functools.partial(attend_kernel, count, first, last),
            out_shape=(packed_shape,) * 4 if last else (stat_shape, acc_shape),
            in_specs=[smem()] + vmem(len(operands) - 1),
            out_specs=tuple(vmem(4 if last else 2)),
            scratch_shapes=[pltpu.VMEM(s.shape, s.dtype) for s in (stat_shape, acc_shape)]
            if last
            else [],
            compiler_params=params(),
            cost_estimate=pl.CostEstimate(
                flops=4 * work * HEAD_DIM, bytes_accessed=3_000_000, transcendentals=work
            ),
            name=f"attend_{index}",
        )(*operands)

    partials = [state[0]]
    for slot, (dy, dc) in enumerate(MATES):
        if slot:
            partials.append(from_frame(state[slot], dy, 0, dc))
    mine = pl.pallas_call(
        merge_kernel,
        out_shape=jax.ShapeDtypeStruct((per_frame, HEAD_DIM), BF16),
        in_specs=vmem(4),
        out_specs=vmem(1)[0],
        compiler_params=params(),
        name="merge",
    )(*partials)

    heads = [mine] + [from_group(mine, a, b) for a, b in SHIFTS[1:]]
    shares = pl.pallas_call(
        mlp_kernel,
        out_shape=(jax.ShapeDtypeStruct((tok, width), F32),)
        + (jax.ShapeDtypeStruct((tok, width), BF16),) * (GROUPS - 1),
        in_specs=[smem()]
        + vmem(2 * GROUPS + 1)
        + [pl.BlockSpec(memory_space=pl.ANY)] * 3,
        out_specs=tuple(vmem(GROUPS)),
        scratch_shapes=[
            pltpu.VMEM((per_frame, GROUPS * HEAD_DIM), BF16),
            pltpu.VMEM((tok, width), F32),
            pltpu.VMEM((per_frame, width), BF16),
            pltpu.VMEM((per_frame, width), F32),
            pltpu.VMEM((GROUPS * HEAD_DIM, width), BF16),
            pltpu.VMEM((width, hidden), BF16),
            pltpu.VMEM((hidden, width), BF16),
            pltpu.SemaphoreType.DMA((3,)),
        ],
        compiler_params=params(),
        name="out_mlp",
    )(place, *heads, *pieces, modulation, w_out_full, w_up, w_down)

    arrived = [
        to_next_frame(share, a, b).astype(F32) for share, (a, b) in zip(shares, SHIFTS)
    ]
    return functools.reduce(lambda p, q: p + q, arrived).astype(BF16)


def solution(mesh):
    return jax.shard_map(
        local,
        mesh=mesh,
        in_specs=(
            P(("frame", "fsdp"), None),
            P("frame"),
            P(),
            P(None, "fsdp"),
            P(),
            P(None, "fsdp"),
            P(None, "fsdp"),
            P(None, "fsdp"),
            P("fsdp"),
            P("fsdp"),
            P("fsdp", None),
            P(None, "fsdp"),
            P("fsdp", None),
        ),
        out_specs=P(("frame", "fsdp"), None),
        check_vma=False,
    )
```

```python
import functools
import math

import jax
import jax.numpy as jnp
from jax import lax
from jax.experimental import pallas as pl
from jax.experimental.pallas import tpu as pltpu
from jax.sharding import PartitionSpec as P

HEAD_DIM = 128
HALF = HEAD_DIM // 2
FREQ = 256
GRID_W = 24
EPS_NORM = 1e-06

Y_HI, Z, CORE = 2, 8, 2
Y_LO, X = 2, 4
FRAMES = Y_HI * Z * CORE
GROUPS = Y_LO * X
SHIFTS = tuple((a, b) for a in range(Y_LO) for b in range(X))
MATES = tuple((dz, dy, dc) for dz in range(2) for dy in range(2) for dc in range(2))
SLOTS = len(MATES)
OFFSETS = (0, 2, -2, 4)
FETCHES = (((0, 1), (0, 3)), ((1, 1), (1, 3)), ((0, 2), (1, 2)))
LOG2E = math.log2(math.e)
NEVER = -1e30
STAT_ROWS = 16
VMEM_LIMIT = 50 * 1024 * 1024

BF16 = jnp.bfloat16
F32 = jnp.float32


def params(limit=VMEM_LIMIT):
    return pltpu.CompilerParams(vmem_limit_bytes=limit)


def vmem(count):
    return [pl.BlockSpec(memory_space=pltpu.VMEM)] * count


def smem():
    return pl.BlockSpec(memory_space=pltpu.SMEM)


def move(array, target):
    pairs = []
    for frame in range(FRAMES):
        for part in range(GROUPS):
            to_frame, to_part = target(frame, part)
            pairs.append((frame * GROUPS + part, to_frame * GROUPS + to_part))
    return lax.ppermute(array, ("frame", "fsdp"), pairs)


def group_shift(part, a, b):
    y, x = divmod(part, X)
    return (y ^ a) * X + (x + b) % X


def frame_shift(frame, dy, dz, dc):
    core = frame % CORE
    z = (frame // CORE) % Z
    y = frame // (CORE * Z)
    return ((y ^ dy) * Z + (z + dz) % Z) * CORE + (core ^ dc)


def from_group(array, a, b):
    return move(array, lambda f, s: (f, group_shift(s, a, -b)))


def from_frame(array, dz):
    return move(array, lambda f, s: (frame_shift(f, 0, -dz, 0), s))


def swapped(array, dz, dy, dc):
    def target(f, s):
        z = (f // CORE) % Z
        return frame_shift(f, dy, (z ^ dz) - z, dc), s

    return move(array, target)


def gathered(array):
    held = {(0, 0): array}
    for a, b in ((0, 1), (1, 3), (0, 3), (1, 1), (1, 0)):
        held[a, b] = from_group(array, a, b)
    held[0, 2] = from_group(held[0, 1], 0, 1)
    held[1, 2] = from_group(held[1, 3], 0, -1)
    return [held[shift] for shift in SHIFTS]


def from_either(array, first, second):
    pairs = []
    for frame in range(FRAMES):
        shift = (first, second)[frame % CORE]
        for part in range(GROUPS):
            if shift is not None:
                source = group_shift(part, *shift)
                pairs.append((frame * GROUPS + source, frame * GROUPS + part))
    return lax.ppermute(array, ("frame", "fsdp"), pairs)


def to_group(array, a, b):
    return move(array, lambda f, s: (f, group_shift(s, a, b)))


def to_next_frame(array, a):
    return move(array, lambda f, s: ((f + 1) % FRAMES, group_shift(s, a, 0)))


def rope_angles(frame_pos, token_pos):
    spatial = HEAD_DIM // 6
    temporal = HALF - 2 * spatial
    pair_index = jnp.arange(HALF, dtype=jnp.int32)
    local_index = jnp.where(
        pair_index < temporal,
        pair_index,
        jnp.where(
            pair_index < temporal + spatial, pair_index - temporal, pair_index - temporal - spatial
        ),
    )
    span = jnp.where(pair_index < temporal, 2 * temporal, 2 * spatial)
    frequency = jnp.exp(-math.log(10000.0) * 2.0 * local_index.astype(F32) / span.astype(F32))
    height = (token_pos // GRID_W).astype(F32)
    across = (token_pos % GRID_W).astype(F32)
    timing = frame_pos.astype(F32)
    index = pair_index[:, None]
    position = jnp.where(
        index < temporal,
        timing[None, :],
        jnp.where(index < temporal + spatial, height[None, :], across[None, :]),
    )
    return position * frequency[:, None]


def normalized(values):
    center = jnp.mean(values, axis=-1, keepdims=True)
    shifted = values - center
    spread = jnp.mean(shifted * shifted, axis=-1, keepdims=True)
    return shifted * lax.rsqrt(spread + EPS_NORM)


def modulation_kernel(level, table, weight, out):
    time = jnp.full((8, FREQ), table[level[0]], jnp.int32).astype(F32)
    halfway = FREQ // 2
    index = lax.broadcasted_iota(jnp.int32, (8, FREQ), 1)
    low = index < halfway
    place = jnp.where(low, index, index - halfway).astype(F32)
    angle = time * jnp.exp(-math.log(10000.0) * place / halfway)
    embedded = jnp.where(low, jnp.cos(angle), jnp.sin(angle))
    active = embedded / (1.0 + jnp.exp(-embedded))
    out[...] = jnp.dot(
        active, weight[...], precision=lax.Precision.HIGHEST, preferred_element_type=F32
    )


def modulation_rows(parts, block_mod, out):
    width, piece = out.shape[1], parts.shape[1]
    step = math.gcd(width, piece)
    for start in range(0, 6 * width, step):
        row, column = divmod(start, width)
        part, offset = divmod(start, piece)
        out[row : row + 1, column : column + step] = (
            parts[part : part + 1, offset : offset + step]
            + block_mod[row : row + 1, column : column + step]
        )


def project_kernel(meta, *refs):
    pieces = refs[:GROUPS]
    parts, block_mod, w_query, w_key, w_value = refs[GROUPS : GROUPS + 5]
    cosine, sine, *gains = refs[GROUPS + 5 : GROUPS + 9]
    query_out, key_out, value_out, squares_out, mod, rows, weights, sems = refs[GROUPS + 9 :]
    copies = [
        pltpu.make_async_copy(source, weights.at[index], sems.at[index])
        for index, source in enumerate((w_value, w_query, w_key))
    ]
    for copy in copies:
        copy.start()
    tok = pieces[0].shape[0]
    modulation_rows(parts, block_mod, mod)
    shift_row = mod[0:1, :]
    scale_row = 1.0 + mod[1:2, :]
    for slot in range(GROUPS):
        values = pieces[slot][...].astype(F32)
        start = pl.multiple_of(meta[slot] * tok, tok)
        rows[pl.ds(start, tok), :] = (normalized(values) * scale_row + shift_row).astype(BF16)
    block = rows[...]
    for copy in copies:
        copy.wait()
    value_raw = jnp.dot(block, weights[0], preferred_element_type=F32)
    value_out[...] = value_raw.astype(BF16)
    found = []
    for kind, out in enumerate((query_out, key_out)):
        raw = jnp.dot(block, weights[1 + kind], preferred_element_type=F32).T
        found.append(jnp.sum(raw * raw, axis=0, keepdims=True))
        raw = raw * jnp.broadcast_to(gains[kind][...], (HEAD_DIM, HEAD_DIM)).T[:, :1]
        first, second = raw[:HALF], raw[HALF:]
        out[:HALF, :] = first * cosine[...] - second * sine[...]
        out[HALF:, :] = first * sine[...] + second * cosine[...]
    per_frame = block.shape[0]
    both = jnp.concatenate(found + [jnp.zeros((6, per_frame), F32)], axis=0)
    for group in range(GROUPS):
        squares_out[group * 8 : group * 8 + 8, :] = both


def scale_kernel(squares, query_raw, key_raw, value_rows, query_out, both_out):
    total = squares[0:8, :]
    for group in range(1, GROUPS):
        total = total + squares[group * 8 : group * 8 + 8, :]
    scale = lax.rsqrt(total / (GROUPS * HEAD_DIM) + EPS_NORM)
    query_out[...] = (query_raw[...] * (scale[0:1] * (LOG2E * HEAD_DIM ** (-0.5)))).astype(BF16)
    tokens = value_rows.shape[0]
    both_out[:tokens, :] = (key_raw[...] * scale[1:2]).T.astype(BF16)
    both_out[tokens:, :] = value_rows[...]


def unpacked(ref):
    parts = ref[HEAD_DIM:, :].astype(F32)
    return ref[:HEAD_DIM, :].astype(F32), parts[0:1] + parts[1:2] + parts[2:3]


def pack(ref, output, level):
    ref[0:HEAD_DIM, :] = output.astype(BF16)
    high = level.astype(BF16).astype(F32)
    middle = (level - high).astype(BF16).astype(F32)
    low = level - high - middle
    filler = jnp.zeros((STAT_ROWS - 3, level.shape[1]), F32)
    ref[HEAD_DIM:, :] = jnp.concatenate([high, middle, low, filler], axis=0).astype(BF16)


def mixed(refs):
    outputs, levels = zip(*[unpacked(ref) for ref in refs])
    highest = functools.reduce(jnp.maximum, levels)
    shares = [jnp.exp2(level - highest) for level in levels]
    total = functools.reduce(lambda p, q: p + q, shares)
    summed = functools.reduce(
        lambda p, q: p + q, [output * share for output, share in zip(outputs, shares)]
    )
    return summed / total, highest + jnp.log2(total)


def attend_kernel(offsets, first, last, meta, *refs):
    blocks = len(offsets)
    query_refs = refs[:SLOTS]
    both_refs = refs[SLOTS : SLOTS + blocks]
    rest = refs[SLOTS + blocks :]
    tokens = query_refs[0].shape[1]
    if not first:
        stat_in, acc_in = rest[:2]
        rest = rest[2:]
    if last:
        packed = rest[:SLOTS]
        stat, acc = rest[SLOTS:]
    else:
        stat, acc = rest
    if first:
        stat[0:SLOTS, :] = jnp.full_like(stat[0:SLOTS, :], NEVER)
        stat[SLOTS:, :] = jnp.zeros_like(stat[SLOTS:, :])
        acc[...] = jnp.zeros_like(acc)
    else:
        stat[...] = stat_in[...]
        acc[...] = acc_in[...]
    for block in range(blocks):
        keys = both_refs[block][:tokens, :]
        values = both_refs[block][tokens:, :]
        for low in range(0, SLOTS, 4):
            all_scores = [
                jnp.dot(keys, query_refs[slot][...], preferred_element_type=F32)
                for slot in range(low, low + 4)
            ]
            for slot, scores in enumerate(all_scores, low):
                rows = slice(slot * HEAD_DIM, (slot + 1) * HEAD_DIM)
                sums = slice(SLOTS + slot, SLOTS + slot + 1)
                seen = meta[GROUPS + SLOTS + offsets[block]] <= meta[GROUPS + slot]
                old_max = stat[slot : slot + 1, :]
                new_max = jnp.maximum(
                    old_max, jnp.where(seen, jnp.max(scores, axis=0, keepdims=True), NEVER)
                )
                decay = jnp.exp2(old_max - new_max)
                probs = jnp.exp2(scores - jnp.where(seen, new_max, -NEVER))
                stat[sums, :] = stat[sums, :] * decay + jnp.sum(probs, axis=0, keepdims=True)
                stat[slot : slot + 1, :] = new_max
                acc[rows, :] = acc[rows, :] * decay + lax.dot_general(
                    values,
                    probs.astype(BF16),
                    (((0,), (0,)), ((), ())),
                    preferred_element_type=F32,
                )

    if last:
        for slot in range(SLOTS):
            total = stat[SLOTS + slot : SLOTS + slot + 1, :]
            seen = total > 0.0
            safe = jnp.where(seen, total, 1.0)
            level = jnp.where(seen, stat[slot : slot + 1, :] + jnp.log2(safe), NEVER)
            rows = slice(slot * HEAD_DIM, (slot + 1) * HEAD_DIM)
            pack(packed[slot], acc[rows, :] / safe, level)


def pair_kernel(*refs):
    halves, outs = refs[:SLOTS], refs[SLOTS:]
    for index, out in enumerate(outs):
        pack(out, *mixed(halves[2 * index : 2 * index + 2]))


def merge_kernel(*refs):
    output, _ = mixed(refs[:-1])
    refs[-1][...] = output.T.astype(BF16)


HIDDEN_STEP = 384


def mlp_kernel(meta, *refs):
    heads = refs[:GROUPS]
    pieces = refs[GROUPS : 2 * GROUPS]
    mod = refs[2 * GROUPS]
    w_outs = refs[2 * GROUPS + 1 : 3 * GROUPS + 1]
    w_up, w_down = refs[3 * GROUPS + 1 : 3 * GROUPS + 3]
    outs = refs[3 * GROUPS + 3 : 3 * GROUPS + 3 + X]
    attended, after, second, total, out_vm, up_vm, down_vm, sems = refs[3 * GROUPS + 3 + X :]
    core = meta[GROUPS + SLOTS + len(OFFSETS)]
    slots = [SHIFTS.index((0, 0)), SHIFTS.index((1, 0))]
    for flip in range(CORE):
        for pair in FETCHES:
            mine, other = SHIFTS.index(pair[flip]), SHIFTS.index(pair[1 - flip])
            slots.append(jnp.where(core == 0, mine, other))
    moves = [
        (source, out_vm.at[pl.ds(pl.multiple_of(slot * HEAD_DIM, HEAD_DIM), HEAD_DIM)])
        for source, slot in zip(w_outs, slots)
    ]
    copies = [
        pltpu.make_async_copy(source, target, sems.at[index])
        for index, (source, target) in enumerate(moves + [(w_up, up_vm), (w_down, down_vm)])
    ]
    for copy in copies:
        copy.start()
    tok = pieces[0].shape[0]
    for slot in range(GROUPS):
        attended[:, slot * HEAD_DIM : (slot + 1) * HEAD_DIM] = heads[slot][...]
    for copy in copies[:-2]:
        copy.wait()
    total[...] = jnp.dot(attended[...], out_vm[...], preferred_element_type=F32)
    gate = mod[2:3, :]
    shift_row = mod[3:4, :]
    scale_row = 1.0 + mod[4:5, :]
    for slot in range(GROUPS):
        rows = pl.ds(pl.multiple_of(meta[slot] * tok, tok), tok)
        summed = pieces[slot][...].astype(F32) + gate * total[rows, :]
        if slot == 0:
            after[...] = summed
        second[rows, :] = (normalized(summed) * scale_row + shift_row).astype(BF16)
    copies[-2].wait()
    hidden = up_vm.shape[0]
    for index, low in enumerate(range(0, hidden, HIDDEN_STEP)):
        high = min(low + HIDDEN_STEP, hidden)
        inner = jax.nn.gelu(
            lax.dot_general(
                second[...],
                up_vm[low:high, :],
                (((1,), (1,)), ((), ())),
                preferred_element_type=F32,
            ),
            approximate=True,
        ).astype(BF16)
        if index == 0:
            copies[-1].wait()
        product = jnp.dot(inner, down_vm[low:high, :], preferred_element_type=F32)
        if index == 0:
            total[...] = product
        else:
            total[...] += product
    last_gate = mod[5:6, :]
    for slot in range(GROUPS):
        rows = pl.ds(pl.multiple_of(meta[slot] * tok, tok), tok)
        share = last_gate * total[rows, :]
        a, b = SHIFTS[slot]
        if slot == 0:
            share = after[...] + share
        outs[b][a * tok : (a + 1) * tok, :] = share.astype(outs[b].dtype)


def local(
    latent_tokens,
    level_index,
    timestep_table,
    time_weight,
    block_mod,
    w_query,
    w_key,
    w_value,
    q_gain,
    k_gain,
    w_out,
    w_up,
    w_down,
):
    frame_id = lax.axis_index("frame")
    part_id = lax.axis_index("fsdp")
    tok, width = latent_tokens.shape
    per_frame = tok * GROUPS
    hidden = w_up.shape[1]
    my_y, my_x = part_id // X, part_id % X
    core = frame_id % CORE
    my_z = (frame_id // CORE) % Z
    my_yhi = frame_id // (CORE * Z)
    places = [(my_y ^ a) * X + (my_x + b) % X for a, b in SHIFTS]
    query_frames = [((my_yhi ^ dy) * Z + (my_z ^ dz)) * CORE + (core ^ dc) for dz, dy, dc in MATES]
    key_frames = [(my_yhi * Z + (my_z + offset) % Z) * CORE + core for offset in OFFSETS]
    meta = jnp.stack(places + query_frames + key_frames + [core]).astype(jnp.int32)

    meta, level_index = lax.optimization_barrier((meta, level_index))
    pieces = gathered(latent_tokens)
    mod_part = pl.pallas_call(
        modulation_kernel,
        out_shape=jax.ShapeDtypeStruct((GROUPS, time_weight.shape[1]), F32),
        in_specs=[smem(), smem()] + vmem(1),
        out_specs=vmem(1)[0],
        compiler_params=params(),
        name="modulation",
    )(level_index, timestep_table, time_weight)
    mod_parts = lax.all_to_all(mod_part, "fsdp", 0, 0, tiled=True)

    token_pos = jnp.arange(per_frame, dtype=jnp.int32)
    angles = rope_angles(jnp.full((per_frame,), frame_id, jnp.int32), token_pos)
    cosine, sine = jnp.cos(angles), jnp.sin(angles)
    w_out, mod_parts, *pieces = lax.optimization_barrier((w_out, mod_parts, *pieces))
    fetched = [from_either(w_out, *pair) for pair in FETCHES[:2]]
    query_raw, key_raw, value_rows, squares, modulation = pl.pallas_call(
        project_kernel,
        out_shape=(
            jax.ShapeDtypeStruct((HEAD_DIM, per_frame), F32),
            jax.ShapeDtypeStruct((HEAD_DIM, per_frame), F32),
            jax.ShapeDtypeStruct((per_frame, HEAD_DIM), BF16),
            jax.ShapeDtypeStruct((GROUPS * 8, per_frame), F32),
            jax.ShapeDtypeStruct((6, width), F32),
        ),
        in_specs=[smem()]
        + vmem(GROUPS + 2)
        + [pl.BlockSpec(memory_space=pltpu.HBM)] * 3
        + vmem(4),
        out_specs=tuple(vmem(5)),
        scratch_shapes=[
            pltpu.VMEM((per_frame, width), BF16),
            pltpu.VMEM((3, width, HEAD_DIM), BF16),
            pltpu.SemaphoreType.DMA((3,)),
        ],
        compiler_params=params(60 * 1024 * 1024),
        name="project",
    )(
        meta,
        *pieces,
        mod_parts,
        block_mod,
        w_query,
        w_key,
        w_value,
        cosine,
        sine,
        q_gain[None, :],
        k_gain[None, :],
    )

    squares = lax.all_to_all(squares, "fsdp", 0, 0, tiled=True)
    squares, w_out, *fetched = lax.optimization_barrier((squares, w_out, *fetched))
    query_t, own_both = pl.pallas_call(
        scale_kernel,
        out_shape=(
            jax.ShapeDtypeStruct((HEAD_DIM, per_frame), BF16),
            jax.ShapeDtypeStruct((2 * per_frame, HEAD_DIM), BF16),
        ),
        in_specs=vmem(4),
        out_specs=tuple(vmem(2)),
        compiler_params=params(60 * 1024 * 1024),
        name="scale",
    )(squares, query_raw, key_raw, value_rows)

    both = [own_both] + [from_frame(own_both, offset) for offset in OFFSETS[1:]]
    queries = []
    for dz, dy, dc in MATES:
        if dc:
            queries.append(swapped(queries[-1], 0, 0, 1))
        elif dz or dy:
            queries.append(swapped(query_t, dz, dy, 0))
        else:
            queries.append(query_t)

    fetched += [from_either(w_out, *FETCHES[2]), from_either(w_out, (1, 0), None)]
    both[-1], *fetched = lax.optimization_barrier((both[-1], *fetched))

    stat_shape = jax.ShapeDtypeStruct((2 * SLOTS, per_frame), F32)
    acc_shape = jax.ShapeDtypeStruct((SLOTS * HEAD_DIM, per_frame), F32)
    packed_shape = jax.ShapeDtypeStruct((HEAD_DIM + STAT_ROWS, per_frame), BF16)
    state = []
    plan = [(0, 1, 2, 3)]
    for index, offsets in enumerate(plan):
        first, last = index == 0, index == len(plan) - 1
        count = len(offsets)
        operands = [meta] + queries + [both[o] for o in offsets] + list(state)
        work = SLOTS * count * per_frame * per_frame
        state = pl.pallas_call(
            functools.partial(attend_kernel, offsets, first, last),
            out_shape=(packed_shape,) * SLOTS if last else (stat_shape, acc_shape),
            in_specs=[smem()] + vmem(len(operands) - 1),
            out_specs=tuple(vmem(SLOTS if last else 2)),
            scratch_shapes=[pltpu.VMEM(s.shape, s.dtype) for s in (stat_shape, acc_shape)]
            if last
            else [],
            compiler_params=params(),
            cost_estimate=pl.CostEstimate(
                flops=4 * work * HEAD_DIM, bytes_accessed=3_000_000, transcendentals=work
            ),
            name=f"attend_{index}",
        )(*operands)

    *fetched, first_packed = lax.optimization_barrier((*fetched, state[0]))
    state = [first_packed, *state[1:]]
    swaps = [swapped(part, 0, 0, 1) for part in fetched]

    halves = []
    for slot in range(0, SLOTS, 2):
        halves += [state[slot], swapped(state[slot + 1], 0, 0, 1)]
    halves[0], *swaps = lax.optimization_barrier((halves[0], *swaps))
    merged = pl.pallas_call(
        pair_kernel,
        out_shape=(packed_shape,) * (SLOTS // 2),
        in_specs=vmem(SLOTS),
        out_specs=tuple(vmem(SLOTS // 2)),
        compiler_params=params(),
        name="merge_cores",
    )(*halves)
    partials = [
        swapped(part, dz, dy, 0) if dz or dy else part
        for part, (dz, dy, dc) in zip(merged, MATES[::2])
    ]
    mate = jnp.where(core == 0, fetched[-1], swaps[-1])
    w_out_pieces = [w_out, mate] + fetched[:-1] + swaps[:-1]
    mine = pl.pallas_call(
        merge_kernel,
        out_shape=jax.ShapeDtypeStruct((per_frame, HEAD_DIM), BF16),
        in_specs=vmem(4),
        out_specs=vmem(1)[0],
        compiler_params=params(),
        name="merge",
    )(*partials)

    heads = gathered(mine)
    shares = pl.pallas_call(
        mlp_kernel,
        out_shape=(jax.ShapeDtypeStruct((Y_LO * tok, width), F32),)
        + (jax.ShapeDtypeStruct((Y_LO * tok, width), BF16),) * (X - 1),
        in_specs=[smem()]
        + vmem(2 * GROUPS + 1)
        + [pl.BlockSpec(memory_space=pl.ANY)] * (GROUPS + 2),
        out_specs=tuple(vmem(X)),
        scratch_shapes=[
            pltpu.VMEM((per_frame, GROUPS * HEAD_DIM), BF16),
            pltpu.VMEM((tok, width), F32),
            pltpu.VMEM((per_frame, width), BF16),
            pltpu.VMEM((per_frame, width), F32),
            pltpu.VMEM((GROUPS * HEAD_DIM, width), BF16),
            pltpu.VMEM((hidden, width), BF16),
            pltpu.VMEM((hidden, width), BF16),
            pltpu.SemaphoreType.DMA((GROUPS + 2,)),
        ],
        compiler_params=params(),
        name="out_mlp",
    )(meta, *heads, *pieces, modulation, *w_out_pieces, w_up.T, w_down)

    arrived = [shares[0]] + [
        to_group(shares[b], 0, b).astype(F32) for b in range(1, X)
    ]
    row = functools.reduce(lambda p, q: p + q, arrived).astype(BF16)
    kept = to_next_frame(row[:tok], 0)
    added = to_next_frame(row[tok:], 1)
    return (kept.astype(F32) + added.astype(F32)).astype(BF16)


def solution(mesh):
    return jax.shard_map(
        local,
        mesh=mesh,
        in_specs=(
            P(("frame", "fsdp"), None),
            P("frame"),
            P(),
            P(None, "fsdp"),
            P(),
            P(None, "fsdp"),
            P(None, "fsdp"),
            P(None, "fsdp"),
            P("fsdp"),
            P("fsdp"),
            P("fsdp", None),
            P(None, "fsdp"),
            P("fsdp", None),
        ),
        out_specs=P(("frame", "fsdp"), None),
        check_vma=False,
    )
```

```python
import functools
import math

import jax
import jax.numpy as jnp
from jax import lax
from jax.experimental import pallas as pl
from jax.experimental.pallas import tpu as pltpu
from jax.sharding import PartitionSpec as P

HEAD_DIM = 128
HALF = HEAD_DIM // 2
FREQ = 256
GRID_W = 24
EPS_NORM = 1e-06

Y_HI, Z, CORE = 2, 8, 2
Y_LO, X = 2, 4
FRAMES = Y_HI * Z * CORE
GROUPS = Y_LO * X
SHIFTS = tuple((a, b) for a in range(Y_LO) for b in range(X))
MATES = tuple((dz, dy, dc) for dz in range(2) for dy in range(2) for dc in range(2))
SLOTS = len(MATES)
OFFSETS = (0, 2, -2, 4)
FETCHES = (((0, 1), (0, 3)), ((1, 1), (1, 3)), ((0, 2), (1, 2)))
LOG2E = math.log2(math.e)
NEVER = -1e30
STAT_ROWS = 16
VMEM_LIMIT = 50 * 1024 * 1024

BF16 = jnp.bfloat16
F32 = jnp.float32


def params(limit=VMEM_LIMIT):
    return pltpu.CompilerParams(vmem_limit_bytes=limit)


def vmem(count):
    return [pl.BlockSpec(memory_space=pltpu.VMEM)] * count


def smem():
    return pl.BlockSpec(memory_space=pltpu.SMEM)


def move(array, target):
    pairs = []
    for frame in range(FRAMES):
        for part in range(GROUPS):
            to_frame, to_part = target(frame, part)
            pairs.append((frame * GROUPS + part, to_frame * GROUPS + to_part))
    return lax.ppermute(array, ("frame", "fsdp"), pairs)


def group_shift(part, a, b):
    y, x = divmod(part, X)
    return (y ^ a) * X + (x + b) % X


def frame_shift(frame, dy, dz, dc):
    core = frame % CORE
    z = (frame // CORE) % Z
    y = frame // (CORE * Z)
    return ((y ^ dy) * Z + (z + dz) % Z) * CORE + (core ^ dc)


def from_group(array, a, b):
    return move(array, lambda f, s: (f, group_shift(s, a, -b)))


def from_frame(array, dz):
    return move(array, lambda f, s: (frame_shift(f, 0, -dz, 0), s))


def swapped(array, dz, dy, dc):
    def target(f, s):
        z = (f // CORE) % Z
        return frame_shift(f, dy, (z ^ dz) - z, dc), s

    return move(array, target)


def gathered(array):
    held = {(0, 0): array}
    for a, b in ((0, 1), (1, 3), (0, 3), (1, 1), (1, 0)):
        held[a, b] = from_group(array, a, b)
    held[0, 2] = from_group(held[0, 1], 0, 1)
    held[1, 2] = from_group(held[1, 3], 0, -1)
    return [held[shift] for shift in SHIFTS]


def from_either(array, first, second):
    pairs = []
    for frame in range(FRAMES):
        shift = (first, second)[frame % CORE]
        for part in range(GROUPS):
            if shift is not None:
                source = group_shift(part, *shift)
                pairs.append((frame * GROUPS + source, frame * GROUPS + part))
    return lax.ppermute(array, ("frame", "fsdp"), pairs)


def to_group(array, a, b):
    return move(array, lambda f, s: (f, group_shift(s, a, b)))


def to_next_frame(array, a):
    return move(array, lambda f, s: ((f + 1) % FRAMES, group_shift(s, a, 0)))


def rope_angles(frame_pos, token_pos):
    spatial = HEAD_DIM // 6
    temporal = HALF - 2 * spatial
    pair_index = jnp.arange(HALF, dtype=jnp.int32)
    local_index = jnp.where(
        pair_index < temporal,
        pair_index,
        jnp.where(
            pair_index < temporal + spatial, pair_index - temporal, pair_index - temporal - spatial
        ),
    )
    span = jnp.where(pair_index < temporal, 2 * temporal, 2 * spatial)
    frequency = jnp.exp(-math.log(10000.0) * 2.0 * local_index.astype(F32) / span.astype(F32))
    height = (token_pos // GRID_W).astype(F32)
    across = (token_pos % GRID_W).astype(F32)
    timing = frame_pos.astype(F32)
    index = pair_index[:, None]
    position = jnp.where(
        index < temporal,
        timing[None, :],
        jnp.where(index < temporal + spatial, height[None, :], across[None, :]),
    )
    return position * frequency[:, None]


def normalized(values):
    center = jnp.mean(values, axis=-1, keepdims=True)
    shifted = values - center
    spread = jnp.mean(shifted * shifted, axis=-1, keepdims=True)
    return shifted * lax.rsqrt(spread + EPS_NORM)


def modulation_kernel(level, table, weight, out):
    time = jnp.full((8, FREQ), table[level[0]], jnp.int32).astype(F32)
    halfway = FREQ // 2
    index = lax.broadcasted_iota(jnp.int32, (8, FREQ), 1)
    low = index < halfway
    place = jnp.where(low, index, index - halfway).astype(F32)
    angle = time * jnp.exp(-math.log(10000.0) * place / halfway)
    embedded = jnp.where(low, jnp.cos(angle), jnp.sin(angle))
    active = embedded / (1.0 + jnp.exp(-embedded))
    out[...] = jnp.dot(
        active, weight[...], precision=lax.Precision.HIGHEST, preferred_element_type=F32
    )


def modulation_rows(parts, block_mod, out):
    width, piece = out.shape[1], parts.shape[1]
    step = math.gcd(width, piece)
    for start in range(0, 6 * width, step):
        row, column = divmod(start, width)
        part, offset = divmod(start, piece)
        out[row : row + 1, column : column + step] = (
            parts[part : part + 1, offset : offset + step]
            + block_mod[row : row + 1, column : column + step]
        )


def project_kernel(meta, *refs):
    pieces = refs[:GROUPS]
    parts, block_mod, w_query, w_key, w_value = refs[GROUPS : GROUPS + 5]
    cosine, sine, *gains = refs[GROUPS + 5 : GROUPS + 9]
    query_out, key_out, value_out, squares_out, mod, rows, weights, sems = refs[GROUPS + 9 :]
    copies = [
        pltpu.make_async_copy(source, weights.at[index], sems.at[index])
        for index, source in enumerate((w_value, w_query, w_key))
    ]
    for copy in copies:
        copy.start()
    tok = pieces[0].shape[0]
    modulation_rows(parts, block_mod, mod)
    shift_row = mod[0:1, :]
    scale_row = 1.0 + mod[1:2, :]
    for slot in range(GROUPS):
        values = pieces[slot][...].astype(F32)
        start = pl.multiple_of(meta[slot] * tok, tok)
        rows[pl.ds(start, tok), :] = (normalized(values) * scale_row + shift_row).astype(BF16)
    block = rows[...]
    for copy in copies:
        copy.wait()
    value_raw = jnp.dot(block, weights[0], preferred_element_type=F32)
    value_out[...] = value_raw.astype(BF16)
    found = []
    for kind, out in enumerate((query_out, key_out)):
        raw = jnp.dot(block, weights[1 + kind], preferred_element_type=F32).T
        found.append(jnp.sum(raw * raw, axis=0, keepdims=True))
        raw = raw * jnp.broadcast_to(gains[kind][...], (HEAD_DIM, HEAD_DIM)).T[:, :1]
        first, second = raw[:HALF], raw[HALF:]
        out[:HALF, :] = first * cosine[...] - second * sine[...]
        out[HALF:, :] = first * sine[...] + second * cosine[...]
    per_frame = block.shape[0]
    both = jnp.concatenate(found + [jnp.zeros((6, per_frame), F32)], axis=0)
    for group in range(GROUPS):
        squares_out[group * 8 : group * 8 + 8, :] = both


def scale_kernel(squares, query_raw, key_raw, value_rows, query_out, both_out):
    total = squares[0:8, :]
    for group in range(1, GROUPS):
        total = total + squares[group * 8 : group * 8 + 8, :]
    scale = lax.rsqrt(total / (GROUPS * HEAD_DIM) + EPS_NORM)
    query_out[...] = (query_raw[...] * (scale[0:1] * (LOG2E * HEAD_DIM ** (-0.5)))).astype(BF16)
    tokens = value_rows.shape[0]
    both_out[:tokens, :] = (key_raw[...] * scale[1:2]).T.astype(BF16)
    both_out[tokens:, :] = value_rows[...]


def unpacked(ref):
    parts = ref[HEAD_DIM:, :].astype(F32)
    return ref[:HEAD_DIM, :].astype(F32), parts[0:1] + parts[1:2] + parts[2:3]


def pack(ref, output, level):
    ref[0:HEAD_DIM, :] = output.astype(BF16)
    high = level.astype(BF16).astype(F32)
    middle = (level - high).astype(BF16).astype(F32)
    low = level - high - middle
    filler = jnp.zeros((STAT_ROWS - 3, level.shape[1]), F32)
    ref[HEAD_DIM:, :] = jnp.concatenate([high, middle, low, filler], axis=0).astype(BF16)


def mixed(refs):
    outputs, levels = zip(*[unpacked(ref) for ref in refs])
    highest = functools.reduce(jnp.maximum, levels)
    shares = [jnp.exp2(level - highest) for level in levels]
    total = functools.reduce(lambda p, q: p + q, shares)
    summed = functools.reduce(
        lambda p, q: p + q, [output * share for output, share in zip(outputs, shares)]
    )
    return summed / total, highest + jnp.log2(total)


def attend_kernel(offsets, first, last, meta, *refs):
    blocks = len(offsets)
    query_refs = refs[:SLOTS]
    both_refs = refs[SLOTS : SLOTS + blocks]
    rest = refs[SLOTS + blocks :]
    tokens = query_refs[0].shape[1]
    if not first:
        stat_in, acc_in = rest[:2]
        rest = rest[2:]
    if last:
        packed = rest[:SLOTS]
        stat, acc = rest[SLOTS:]
    else:
        stat, acc = rest
    if first:
        stat[0:SLOTS, :] = jnp.full_like(stat[0:SLOTS, :], NEVER)
        stat[SLOTS:, :] = jnp.zeros_like(stat[SLOTS:, :])
        acc[...] = jnp.zeros_like(acc)
    else:
        stat[...] = stat_in[...]
        acc[...] = acc_in[...]
    for block in range(blocks):
        keys = both_refs[block][:tokens, :]
        values = both_refs[block][tokens:, :]
        for low in range(0, SLOTS, 4):
            all_scores = [
                jnp.dot(keys, query_refs[slot][...], preferred_element_type=F32)
                for slot in range(low, low + 4)
            ]
            for slot, scores in enumerate(all_scores, low):
                rows = slice(slot * HEAD_DIM, (slot + 1) * HEAD_DIM)
                sums = slice(SLOTS + slot, SLOTS + slot + 1)
                seen = meta[GROUPS + SLOTS + offsets[block]] <= meta[GROUPS + slot]
                old_max = stat[slot : slot + 1, :]
                new_max = jnp.maximum(
                    old_max, jnp.where(seen, jnp.max(scores, axis=0, keepdims=True), NEVER)
                )
                decay = jnp.exp2(old_max - new_max)
                probs = jnp.exp2(scores - jnp.where(seen, new_max, -NEVER))
                stat[sums, :] = stat[sums, :] * decay + jnp.sum(probs, axis=0, keepdims=True)
                stat[slot : slot + 1, :] = new_max
                acc[rows, :] = acc[rows, :] * decay + lax.dot_general(
                    values,
                    probs.astype(BF16),
                    (((0,), (0,)), ((), ())),
                    preferred_element_type=F32,
                )

    if last:
        for slot in range(SLOTS):
            total = stat[SLOTS + slot : SLOTS + slot + 1, :]
            seen = total > 0.0
            safe = jnp.where(seen, total, 1.0)
            level = jnp.where(seen, stat[slot : slot + 1, :] + jnp.log2(safe), NEVER)
            rows = slice(slot * HEAD_DIM, (slot + 1) * HEAD_DIM)
            pack(packed[slot], acc[rows, :] / safe, level)


def pair_kernel(*refs):
    halves, outs = refs[:SLOTS], refs[SLOTS:]
    for index, out in enumerate(outs):
        pack(out, *mixed(halves[2 * index : 2 * index + 2]))


def merge_kernel(*refs):
    output, _ = mixed(refs[:-1])
    refs[-1][...] = output.T.astype(BF16)


HIDDEN_STEP = 384


def mlp_kernel(meta, *refs):
    heads = refs[:GROUPS]
    pieces = refs[GROUPS : 2 * GROUPS]
    mod = refs[2 * GROUPS]
    w_outs = refs[2 * GROUPS + 1 : 3 * GROUPS + 1]
    w_up, w_down = refs[3 * GROUPS + 1 : 3 * GROUPS + 3]
    outs = refs[3 * GROUPS + 3 : 3 * GROUPS + 3 + X]
    attended, after, second, total, out_vm, up_vm, down_vm, sems = refs[3 * GROUPS + 3 + X :]
    core = meta[GROUPS + SLOTS + len(OFFSETS)]
    slots = [SHIFTS.index((0, 0)), SHIFTS.index((1, 0))]
    for flip in range(CORE):
        for pair in FETCHES:
            mine, other = SHIFTS.index(pair[flip]), SHIFTS.index(pair[1 - flip])
            slots.append(jnp.where(core == 0, mine, other))
    moves = [
        (source, out_vm.at[pl.ds(pl.multiple_of(slot * HEAD_DIM, HEAD_DIM), HEAD_DIM)])
        for source, slot in zip(w_outs, slots)
    ]
    copies = [
        pltpu.make_async_copy(source, target, sems.at[index])
        for index, (source, target) in enumerate(moves + [(w_up, up_vm), (w_down, down_vm)])
    ]
    for copy in copies:
        copy.start()
    tok = pieces[0].shape[0]
    for slot in range(GROUPS):
        attended[:, slot * HEAD_DIM : (slot + 1) * HEAD_DIM] = heads[slot][...]
    for copy in copies[:-2]:
        copy.wait()
    total[...] = jnp.dot(attended[...], out_vm[...], preferred_element_type=F32)
    gate = mod[2:3, :]
    shift_row = mod[3:4, :]
    scale_row = 1.0 + mod[4:5, :]
    for slot in range(GROUPS):
        rows = pl.ds(pl.multiple_of(meta[slot] * tok, tok), tok)
        summed = pieces[slot][...].astype(F32) + gate * total[rows, :]
        if slot == 0:
            after[...] = summed
        second[rows, :] = (normalized(summed) * scale_row + shift_row).astype(BF16)
    copies[-2].wait()
    hidden = up_vm.shape[0]
    for index, low in enumerate(range(0, hidden, HIDDEN_STEP)):
        high = min(low + HIDDEN_STEP, hidden)
        inner = jax.nn.gelu(
            lax.dot_general(
                second[...],
                up_vm[low:high, :],
                (((1,), (1,)), ((), ())),
                preferred_element_type=F32,
            ),
            approximate=True,
        ).astype(BF16)
        if index == 0:
            copies[-1].wait()
        product = jnp.dot(inner, down_vm[low:high, :], preferred_element_type=F32)
        if index == 0:
            total[...] = product
        else:
            total[...] += product
    last_gate = mod[5:6, :]
    for slot in range(GROUPS):
        rows = pl.ds(pl.multiple_of(meta[slot] * tok, tok), tok)
        share = last_gate * total[rows, :]
        a, b = SHIFTS[slot]
        if slot == 0:
            share = after[...] + share
        outs[b][a * tok : (a + 1) * tok, :] = share.astype(outs[b].dtype)


def local(
    latent_tokens,
    level_index,
    timestep_table,
    time_weight,
    block_mod,
    w_query,
    w_key,
    w_value,
    q_gain,
    k_gain,
    w_out,
    w_up,
    w_down,
):
    frame_id = lax.axis_index("frame")
    part_id = lax.axis_index("fsdp")
    tok, width = latent_tokens.shape
    per_frame = tok * GROUPS
    hidden = w_up.shape[1]
    my_y, my_x = part_id // X, part_id % X
    core = frame_id % CORE
    my_z = (frame_id // CORE) % Z
    my_yhi = frame_id // (CORE * Z)
    places = [(my_y ^ a) * X + (my_x + b) % X for a, b in SHIFTS]
    query_frames = [((my_yhi ^ dy) * Z + (my_z ^ dz)) * CORE + (core ^ dc) for dz, dy, dc in MATES]
    key_frames = [(my_yhi * Z + (my_z + offset) % Z) * CORE + core for offset in OFFSETS]
    meta = jnp.stack(places + query_frames + key_frames + [core]).astype(jnp.int32)

    meta, level_index = lax.optimization_barrier((meta, level_index))
    pieces = gathered(latent_tokens)
    mod_part = pl.pallas_call(
        modulation_kernel,
        out_shape=jax.ShapeDtypeStruct((GROUPS, time_weight.shape[1]), F32),
        in_specs=[smem(), smem()] + vmem(1),
        out_specs=vmem(1)[0],
        compiler_params=params(),
        name="modulation",
    )(level_index, timestep_table, time_weight)
    mod_parts = lax.all_to_all(mod_part, "fsdp", 0, 0, tiled=True)

    token_pos = jnp.arange(per_frame, dtype=jnp.int32)
    angles = rope_angles(jnp.full((per_frame,), frame_id, jnp.int32), token_pos)
    cosine, sine = jnp.cos(angles), jnp.sin(angles)
    w_out, mod_parts, *pieces = lax.optimization_barrier((w_out, mod_parts, *pieces))
    fetched = [from_either(w_out, *pair) for pair in FETCHES[:2]]
    query_raw, key_raw, value_rows, squares, modulation = pl.pallas_call(
        project_kernel,
        out_shape=(
            jax.ShapeDtypeStruct((HEAD_DIM, per_frame), F32),
            jax.ShapeDtypeStruct((HEAD_DIM, per_frame), F32),
            jax.ShapeDtypeStruct((per_frame, HEAD_DIM), BF16),
            jax.ShapeDtypeStruct((GROUPS * 8, per_frame), F32),
            jax.ShapeDtypeStruct((6, width), F32),
        ),
        in_specs=[smem()]
        + vmem(GROUPS + 2)
        + [pl.BlockSpec(memory_space=pltpu.HBM)] * 3
        + vmem(4),
        out_specs=tuple(vmem(5)),
        scratch_shapes=[
            pltpu.VMEM((per_frame, width), BF16),
            pltpu.VMEM((3, width, HEAD_DIM), BF16),
            pltpu.SemaphoreType.DMA((3,)),
        ],
        compiler_params=params(60 * 1024 * 1024),
        name="project",
    )(
        meta,
        *pieces,
        mod_parts,
        block_mod,
        w_query,
        w_key,
        w_value,
        cosine,
        sine,
        q_gain[None, :],
        k_gain[None, :],
    )

    squares = lax.all_to_all(squares, "fsdp", 0, 0, tiled=True)
    squares, w_out, *fetched = lax.optimization_barrier((squares, w_out, *fetched))
    query_t, own_both = pl.pallas_call(
        scale_kernel,
        out_shape=(
            jax.ShapeDtypeStruct((HEAD_DIM, per_frame), BF16),
            jax.ShapeDtypeStruct((2 * per_frame, HEAD_DIM), BF16),
        ),
        in_specs=vmem(4),
        out_specs=tuple(vmem(2)),
        compiler_params=params(60 * 1024 * 1024),
        name="scale",
    )(squares, query_raw, key_raw, value_rows)

    both = [own_both] + [from_frame(own_both, offset) for offset in OFFSETS[1:]]
    queries = []
    for dz, dy, dc in MATES:
        if dc:
            queries.append(swapped(queries[-1], 0, 0, 1))
        elif dz or dy:
            queries.append(swapped(query_t, dz, dy, 0))
        else:
            queries.append(query_t)

    stat_shape = jax.ShapeDtypeStruct((2 * SLOTS, per_frame), F32)
    acc_shape = jax.ShapeDtypeStruct((SLOTS * HEAD_DIM, per_frame), F32)
    packed_shape = jax.ShapeDtypeStruct((HEAD_DIM + STAT_ROWS, per_frame), BF16)
    state = []
    plan = [(0,), (1, 2), (3,)]
    for index, offsets in enumerate(plan):
        first, last = index == 0, index == len(plan) - 1
        count = len(offsets)
        operands = [meta] + queries + [both[o] for o in offsets] + list(state)
        work = SLOTS * count * per_frame * per_frame
        state = pl.pallas_call(
            functools.partial(attend_kernel, offsets, first, last),
            out_shape=(packed_shape,) * SLOTS if last else (stat_shape, acc_shape),
            in_specs=[smem()] + vmem(len(operands) - 1),
            out_specs=tuple(vmem(SLOTS if last else 2)),
            scratch_shapes=[pltpu.VMEM(s.shape, s.dtype) for s in (stat_shape, acc_shape)]
            if last
            else [],
            compiler_params=params(),
            cost_estimate=pl.CostEstimate(
                flops=4 * work * HEAD_DIM, bytes_accessed=3_000_000, transcendentals=work
            ),
            name=f"attend_{index}",
        )(*operands)
        if index == 0:
            w_out, *state = lax.optimization_barrier((w_out, *state))
            late = [from_either(w_out, *FETCHES[2]), from_either(w_out, (1, 0), None)]
        elif index == 1:
            *fetched, stat_now, acc_now = lax.optimization_barrier((*fetched, *state))
            state = [stat_now, acc_now]
            swaps = [swapped(part, 0, 0, 1) for part in fetched]

    halves = []
    for slot in range(0, SLOTS, 2):
        halves += [state[slot], swapped(state[slot + 1], 0, 0, 1)]
    halves[0], *swaps = lax.optimization_barrier((halves[0], *swaps))
    merged = pl.pallas_call(
        pair_kernel,
        out_shape=(packed_shape,) * (SLOTS // 2),
        in_specs=vmem(SLOTS),
        out_specs=tuple(vmem(SLOTS // 2)),
        compiler_params=params(),
        name="merge_cores",
    )(*halves)
    *late, kept = lax.optimization_barrier((*late, merged[0]))
    merged = (kept, *merged[1:])
    late_swaps = [swapped(part, 0, 0, 1) for part in late]
    partials = [
        swapped(part, dz, dy, 0) if dz or dy else part
        for part, (dz, dy, dc) in zip(merged, MATES[::2])
    ]
    partials[0], *late_swaps = lax.optimization_barrier((partials[0], *late_swaps))
    fetched, swaps = fetched + late, swaps + late_swaps
    mate = jnp.where(core == 0, fetched[-1], swaps[-1])
    w_out_pieces = [w_out, mate] + fetched[:-1] + swaps[:-1]
    mine = pl.pallas_call(
        merge_kernel,
        out_shape=jax.ShapeDtypeStruct((per_frame, HEAD_DIM), BF16),
        in_specs=vmem(4),
        out_specs=vmem(1)[0],
        compiler_params=params(),
        name="merge",
    )(*partials)

    heads = gathered(mine)
    shares = pl.pallas_call(
        mlp_kernel,
        out_shape=(jax.ShapeDtypeStruct((Y_LO * tok, width), F32),)
        + (jax.ShapeDtypeStruct((Y_LO * tok, width), BF16),) * (X - 1),
        in_specs=[smem()]
        + vmem(2 * GROUPS + 1)
        + [pl.BlockSpec(memory_space=pl.ANY)] * (GROUPS + 2),
        out_specs=tuple(vmem(X)),
        scratch_shapes=[
            pltpu.VMEM((per_frame, GROUPS * HEAD_DIM), BF16),
            pltpu.VMEM((tok, width), F32),
            pltpu.VMEM((per_frame, width), BF16),
            pltpu.VMEM((per_frame, width), F32),
            pltpu.VMEM((GROUPS * HEAD_DIM, width), BF16),
            pltpu.VMEM((hidden, width), BF16),
            pltpu.VMEM((hidden, width), BF16),
            pltpu.SemaphoreType.DMA((GROUPS + 2,)),
        ],
        compiler_params=params(),
        name="out_mlp",
    )(meta, *heads, *pieces, modulation, *w_out_pieces, w_up.T, w_down)

    arrived = [shares[0]] + [
        to_group(shares[b], 0, b).astype(F32) for b in range(1, X)
    ]
    row = functools.reduce(lambda p, q: p + q, arrived).astype(BF16)
    kept = to_next_frame(row[:tok], 0)
    added = to_next_frame(row[tok:], 1)
    return (kept.astype(F32) + added.astype(F32)).astype(BF16)


def solution(mesh):
    return jax.shard_map(
        local,
        mesh=mesh,
        in_specs=(
            P(("frame", "fsdp"), None),
            P("frame"),
            P(),
            P(None, "fsdp"),
            P(),
            P(None, "fsdp"),
            P(None, "fsdp"),
            P(None, "fsdp"),
            P("fsdp"),
            P("fsdp"),
            P("fsdp", None),
            P(None, "fsdp"),
            P("fsdp", None),
        ),
        out_specs=P(("frame", "fsdp"), None),
        check_vma=False,
    )
```
